32 devices in a mesh: rep: 1, node: 32 (over z, y, x, core).
Axes of the slice: x: 2, y: 2, z: 4, core: 2. Of those that a mesh axis runs over, the one named last changes fastest.
Arguments:
- tokens: bfloat16 [2048, 7168], P(('rep', 'node')), may hold values from -6 to 6
- routes: int32 [2048, 2], P(('rep', 'node')), may hold values from 0 to 3, all different within a row; in each aligned block of 64 rows (0 to 63, 64 to 127, ...) at most 64 rows name the same one
- probs: float32 [2048, 2], P(('rep', 'node')), may hold values from 0.2 to 1
- w_gate: bfloat16 [32, 7168, 256], P('node'), may hold values from -0.0625 to 0.0625
- w_up: bfloat16 [32, 7168, 256], P('node'), may hold values from -0.0625 to 0.0625
- w_down: bfloat16 [32, 256, 7168], P('node'), may hold values from -0.125 to 0.125
Outputs:
- mixed: bfloat16 [2048, 7168], P(('rep', 'node'))
The draws below stay inside these ranges and needn't reach their ends.
Inputs may be any that keep to these rules, and one draw needn't show every extreme that they name: `routes`: each token names 2 different experts; the tokens held by one device name no expert more than 64 times, and in every draw some expert exactly 64 times.
All inputs are finite; a program needn't handle non-finite values.
Results may differ from the reference program's by a relative error of at most 0.0057.
Values may be sent and summed in bfloat16 or wider, within the bound.
No kernel may reach another device: no remote copies, remote signals or barrier semaphores. Data moves between devices by JAX's collectives and lax.ppermute only.
A program may use at most 256 MiB of HBM per device.

```python
import math
import jax
import jax.numpy as jnp
import numpy as np
from jax import lax

D = 7168
FF = 2048
GROUP = 8
TOPK = 2
TOK_DEV = 64
SLICE = 256
EXPERTS = 4
TOKENS = 2048
CAP = 64
N_NODE = 32


def block_scale(key, dims, cuts, low, top_value):
    gain = 1.0
    for position, blocks in cuts:
        steps = jax.random.uniform(jax.random.fold_in(jax.random.fold_in(key, 6), position), (blocks,), jnp.float32, low / len(cuts), top_value / len(cuts))
        gain = gain * jnp.repeat(jnp.exp(steps), dims[position] // blocks).reshape((-1,) + (1,) * (len(dims) - 1 - position))
    return gain


def deal_out(key, own, number, rows, number_of, top, bound, lean):
    sequence = jax.random.permutation(key, number_of)
    heavy_load, common = portions_of(number_of, rows * top, bound, lean, True), portions_of(number_of, rows * top, bound, lean, False)
    places = jnp.arange(number_of)

    def named(sizes, offset_by):
        used = int((sizes > 0).sum())
        fixed = max(1, used // 4)
        passed = fixed + (places - fixed + offset_by * (used - fixed)) % max(1, number_of - fixed)
        return jnp.zeros((number_of,), jnp.int32).at[sequence[jnp.where(places < fixed, places, passed)]].set(jnp.asarray(sizes, jnp.int32))

    sizes = jnp.where(number % 4 == 0, named(heavy_load, number // 4), named(common, number - number // 4 - 1))
    mixed = jax.random.permutation(jax.random.fold_in(own, 3), number_of)
    giver, sink = mixed[0:number_of // 2 * 2:2], mixed[1:number_of // 2 * 2:2]
    slack = jnp.minimum(sizes[giver] - 1, bound - sizes[sink]) // 2
    slack = jnp.where((giver == sequence[0]) | (sink == sequence[0]) | (sizes[sink] == 0), 0, jnp.maximum(slack, 0))
    passed = jax.random.randint(jax.random.fold_in(own, 4), (number_of // 2,), 0, 1 << 20) % (slack + 1)
    sizes = sizes.at[giver].add(-passed).at[sink].add(passed)
    members = jnp.searchsorted(jnp.cumsum(sizes), jnp.arange(rows * top), side="right").astype(jnp.int32)
    grid = members.reshape(top, rows).T
    grid = grid[jax.random.permutation(jax.random.fold_in(own, 1), rows)]
    offset_by = jax.random.randint(jax.random.fold_in(own, 2), (rows, 1), 0, top)
    return jnp.take_along_axis(grid, (jnp.arange(top)[None, :] + offset_by) % top, axis=1)


def portions_of(number_of, total, most, lean, full):
    weights = [(1 << 20) // math.isqrt(grade ** lean) + 1 for grade in range(1, number_of + 1)]
    largest = most if full else min(most, max(-(-total // number_of), total * weights[0] // sum(weights)))
    least = 1 if total - largest >= number_of - 1 else 0
    counts, surplus = [largest] + [least] * (number_of - 1), total - largest - least * (number_of - 1)
    while surplus > 0:
        movable = [i for i in range(1, number_of) if counts[i] < largest] or [i for i in range(1, number_of) if counts[i] < most]
        whole, left = sum([weights[i] for i in movable]), surplus
        for i in movable:
            more = min(most - counts[i], max(1, left * weights[i] // whole), surplus)
            counts[i] = counts[i] + more
            surplus = surplus - more
    return np.array(counts)


def gaussian(own_key, shape, width, bound, cuts=(), kind=jnp.bfloat16):
    level = block_scale(own_key, shape, cuts, -0.22, 0.18) if cuts else 1.0
    drawn = jax.random.normal(own_key, shape, jnp.float32) * width * level
    return jnp.minimum(jnp.maximum(drawn, -bound), bound).astype(kind)


def setup_inputs(seed: int = 0, part: int = 0) -> dict:
    arg_keys = jax.random.split(jax.random.key(seed), 7)
    part_splits = jax.random.split(jax.random.fold_in(arg_keys[6], part), 7)
    tokens = gaussian(part_splits[0], (TOKENS, D), 1.0, 6.0, ((0, 32),))
    routes_keys = jax.random.split(jax.random.fold_in(part_splits[1], 1), TOKENS // TOK_DEV)
    routes_turns = jax.random.permutation(jax.random.fold_in(part_splits[1], 3), TOKENS // TOK_DEV)
    routes = jax.vmap(lambda own, number: deal_out(jax.random.fold_in(part_splits[1], 2), own, number, TOK_DEV, EXPERTS, TOPK, CAP, 2))(routes_keys, routes_turns).reshape((TOKENS, TOPK))
    probs = jnp.clip(jnp.exp(math.log(1.0) - 1.609438 * jax.random.uniform(part_splits[2], (TOKENS, TOPK), jnp.float32) ** block_scale(part_splits[2], (TOKENS, TOPK), ((0, 32),), -0.2, 0.2)), 0.2, 1.0)
    w_gate = gaussian(arg_keys[3], (EXPERTS * GROUP, D, SLICE), D ** -0.5, 0.0625, ((0, 32),))
    w_up = gaussian(arg_keys[4], (EXPERTS * GROUP, D, SLICE), D ** -0.5, 0.0625, ((0, 32),))
    w_down = gaussian(arg_keys[5], (EXPERTS * GROUP, SLICE, D), FF ** -0.5, 0.125, ((0, 32),))
    return {"tokens": tokens, "routes": routes, "probs": probs, "w_gate": w_gate, "w_up": w_up, "w_down": w_down}


def reference(tokens, routes, probs, w_gate, w_up, w_down):
    rows = N_NODE * CAP
    gate_all = w_gate.reshape(EXPERTS, GROUP, D, SLICE)
    up_all = w_up.reshape(EXPERTS, GROUP, D, SLICE)
    down_all = w_down.reshape(EXPERTS, FF, D)

    def per_expert(total, item):
        gate_e, up_e, down_e, expert = item
        gate_w = jnp.transpose(gate_e, (1, 0, 2)).reshape(D, FF)
        up_w = jnp.transpose(up_e, (1, 0, 2)).reshape(D, FF)
        struck = routes == expert
        weight = jnp.sum(jnp.where(struck, probs, jnp.zeros_like(probs)), axis=1)
        keyed = jnp.where(jnp.any(struck, axis=1), 0, 1).astype(jnp.int32)
        order = jnp.argsort(keyed, stable=True)[:rows].astype(jnp.int32)
        chosen = tokens[order]
        gate = jnp.dot(chosen, gate_w, preferred_element_type=jnp.float32)
        up = jnp.dot(chosen, up_w, preferred_element_type=jnp.float32)
        hidden = (jax.nn.silu(gate) * up).astype(jnp.bfloat16)
        result = jnp.dot(hidden, down_e, preferred_element_type=jnp.float32).astype(jnp.bfloat16)
        total = total.at[order].add(weight[order][:, None] * result.astype(total.dtype))
        return total, None

    start = jnp.zeros((TOKENS, D), jnp.float32)
    total, unused = lax.scan(per_expert, start, (gate_all, up_all, down_all, jnp.arange(EXPERTS, dtype=jnp.int32)))
    return total.astype(jnp.bfloat16)
```

```python
import jax
import jax.numpy as jnp
from jax import lax
from jax.sharding import PartitionSpec as P

GROUP = 8
PLANES = 4


def general(tokens, routes, probs, w_gate, w_up, w_down):
    tok_rows, width = tokens.shape
    chosen_count = routes.shape[1]
    devices = lax.axis_size("node")
    experts = devices // GROUP
    slots = min(tok_rows, GROUP * max(1, 2 * tok_rows * chosen_count // (experts * GROUP)))
    flat_routes = routes.reshape(-1)
    onehot = (flat_routes[:, None] == jnp.arange(experts, dtype=jnp.int32)[None, :]).astype(
        jnp.int32
    )
    ranks = jnp.sum((jnp.cumsum(onehot, axis=0) - onehot) * onehot, axis=1)
    target = flat_routes * slots + ranks
    placed = target[:, None] == jnp.arange(experts * slots, dtype=jnp.int32)[None, :]
    placed = placed.reshape(tok_rows, chosen_count, experts * slots)
    sender = jnp.sum(placed.astype(jnp.float32), axis=1).astype(jnp.bfloat16)
    combine = jnp.sum(jnp.where(placed, probs[:, :, None], 0.0), axis=1)
    packed = lax.dot_general(
        sender, tokens, (((0,), (0,)), ((), ())), preferred_element_type=jnp.float32
    ).astype(jnp.bfloat16)
    spread = jnp.broadcast_to(
        packed.reshape(experts, 1, slots, width), (experts, GROUP, slots, width)
    )
    spread = spread.reshape(devices, slots, width)
    block = lax.all_to_all(spread, "node", split_axis=0, concat_axis=0, tiled=True)
    lead = block.shape[:-1]
    flat_rows = block.reshape(-1, width)
    gate = jnp.dot(flat_rows, w_gate[0], preferred_element_type=jnp.float32)
    up = jnp.dot(flat_rows, w_up[0], preferred_element_type=jnp.float32)
    hidden = (jax.nn.silu(gate) * up).astype(jnp.bfloat16)
    returned = lax.all_to_all(
        jnp.dot(hidden, w_down[0], preferred_element_type=jnp.float32).reshape(lead + (width,)),
        "node",
        split_axis=0,
        concat_axis=0,
        tiled=True,
    )
    summed = jnp.sum(returned.reshape(experts, GROUP, slots, width), axis=1).astype(jnp.bfloat16)
    mixed = jnp.dot(
        combine,
        summed.reshape(experts * slots, width).astype(jnp.float32),
        precision=lax.Precision.HIGHEST,
    )
    return mixed.astype(jnp.bfloat16)


CORE, X, Y, Z = 1, 2, 4, 8
COUNT = PLANES * GROUP


def swap(value, bits):
    return lax.ppermute(value, "node", [(i, i ^ bits) for i in range(COUNT)])


def shift(value, step, planes):
    return lax.ppermute(
        value,
        "node",
        [(z * GROUP + m, (z + step) * GROUP + m) for z in planes for m in range(GROUP)],
    )


def plane_gather(own):
    rows = own.shape[0] // 2
    by_x = swap(own, X)
    by_y = swap(own, Y)
    low = swap(by_x[:rows], Y)
    high = swap(by_y[rows:], X)
    return own, by_x, by_y, jnp.concatenate([low, high], axis=0)


def after(value, *earlier):
    return lax.optimization_barrier((value,) + earlier)[0]


def four_planes(tokens, routes, probs, w_gate, w_up, w_down):
    rows, width = tokens.shape
    part = width // 4
    me = lax.axis_index("node")
    z = me // GROUP
    quarter = me // 2 % 4

    gate_w = jnp.concatenate([w_gate[0], swap(w_gate[0], CORE)], axis=1)
    up_w = jnp.concatenate([w_up[0], swap(w_up[0], CORE)], axis=1)

    def cut(r):
        return lax.dynamic_slice_in_dim(w_down[0], (quarter ^ r) * part, part, axis=1)

    up1 = shift(tokens, 1, (0, 1, 2))
    dn1 = shift(tokens, -1, (1, 2, 3))
    up2 = shift(up1, 1, (1, 2))
    dn2 = shift(dn1, -1, (1, 2))
    up3 = shift(up2, 1, (2,))
    dn3 = shift(dn2, -1, (1,))
    columns = [
        tokens,
        jnp.where(z % 2 == 0, dn1, up1),
        jnp.where(z < 2, dn2, up2),
        jnp.where(z == 0, dn3, jnp.where(z == 1, dn1, jnp.where(z == 2, up1, up3))),
    ]

    down_x = swap(cut(1), X)
    down_y = swap(cut(2), Y)
    down_d = swap(cut(3), X + Y)
    down_mine = jnp.stack([cut(0), down_x, down_y, down_d])
    down_other = swap(down_mine, CORE)
    down_w = jnp.concatenate([down_mine, down_other], axis=1).reshape(-1, part)

    experts = jnp.arange(PLANES, dtype=jnp.int32)
    weights = jnp.sum(
        jnp.where(routes[:, :, None] == experts, probs[:, :, None], 0.0), axis=1
    )
    weights = jnp.concatenate(
        [weights, swap(weights, X), swap(weights, Y), swap(weights, X + Y)], axis=0
    )

    def weight_of(k):
        return jnp.sum(jnp.where(experts == (z ^ k), weights, 0.0), axis=1, keepdims=True)

    total = None
    for k in (1, 2, 3, 0):
        block = jnp.concatenate(plane_gather(columns[k]), axis=0)
        gate = jnp.dot(block, gate_w, preferred_element_type=jnp.float32)
        up = jnp.dot(block, up_w, preferred_element_type=jnp.float32)
        hidden = (jax.nn.silu(gate) * up).astype(jnp.bfloat16)
        units = [u.reshape(4, rows, -1) for u in plane_gather(hidden)]
        hidden = jnp.concatenate(
            [jnp.concatenate([units[r][j ^ r] for j in range(4)], axis=0) for r in range(4)],
            axis=1,
        )
        out = jnp.dot(hidden, down_w, preferred_element_type=jnp.float32).astype(jnp.bfloat16)
        if k:
            out = swap(out, k * Z)
        term = weight_of(k) * out.astype(jnp.float32)
        total = term if total is None else total + term
    mixed = total.astype(jnp.bfloat16).reshape(4, rows, part)
    pieces = [mixed[0], swap(mixed[1], X), swap(mixed[2], Y), swap(mixed[3], X + Y)]
    result = []
    for a in range(4):
        piece = pieces[a]
        for q in range(1, 4):
            piece = jnp.where(quarter == q, pieces[a ^ q], piece)
        result.append(piece)
    return jnp.concatenate(result, axis=1)


def solution(mesh):
    devices = mesh.shape["node"]

    def per_device(tokens, routes, probs, w_gate, w_up, w_down):
        path = four_planes if devices == COUNT else general
        return path(tokens, routes, probs, w_gate, w_up, w_down)

    in_specs = (
        P(("rep", "node"), None),
        P(("rep", "node"), None),
        P(("rep", "node"), None),
        P("node", None, None),
        P("node", None, None),
        P("node", None, None),
    )
    out_specs = P(("rep", "node"), None)
    return jax.shard_map(
        per_device, mesh=mesh, in_specs=in_specs, out_specs=out_specs, check_vma=False
    )
```

```python
import jax
import jax.numpy as jnp
from jax import lax
from jax.experimental import pallas as pl
from jax.experimental.pallas import tpu as pltpu
from jax.sharding import PartitionSpec as P

GROUP = 8
PLANES = 4


def general(tokens, routes, probs, w_gate, w_up, w_down):
    tok_rows, width = tokens.shape
    chosen_count = routes.shape[1]
    devices = lax.axis_size("node")
    experts = devices // GROUP
    slots = min(tok_rows, GROUP * max(1, 2 * tok_rows * chosen_count // (experts * GROUP)))
    flat_routes = routes.reshape(-1)
    onehot = (flat_routes[:, None] == jnp.arange(experts, dtype=jnp.int32)[None, :]).astype(
        jnp.int32
    )
    ranks = jnp.sum((jnp.cumsum(onehot, axis=0) - onehot) * onehot, axis=1)
    target = flat_routes * slots + ranks
    placed = target[:, None] == jnp.arange(experts * slots, dtype=jnp.int32)[None, :]
    placed = placed.reshape(tok_rows, chosen_count, experts * slots)
    sender = jnp.sum(placed.astype(jnp.float32), axis=1).astype(jnp.bfloat16)
    combine = jnp.sum(jnp.where(placed, probs[:, :, None], 0.0), axis=1)
    packed = lax.dot_general(
        sender, tokens, (((0,), (0,)), ((), ())), preferred_element_type=jnp.float32
    ).astype(jnp.bfloat16)
    spread = jnp.broadcast_to(
        packed.reshape(experts, 1, slots, width), (experts, GROUP, slots, width)
    )
    spread = spread.reshape(devices, slots, width)
    block = lax.all_to_all(spread, "node", split_axis=0, concat_axis=0, tiled=True)
    lead = block.shape[:-1]
    flat_rows = block.reshape(-1, width)
    gate = jnp.dot(flat_rows, w_gate[0], preferred_element_type=jnp.float32)
    up = jnp.dot(flat_rows, w_up[0], preferred_element_type=jnp.float32)
    hidden = (jax.nn.silu(gate) * up).astype(jnp.bfloat16)
    returned = lax.all_to_all(
        jnp.dot(hidden, w_down[0], preferred_element_type=jnp.float32).reshape(lead + (width,)),
        "node",
        split_axis=0,
        concat_axis=0,
        tiled=True,
    )
    summed = jnp.sum(returned.reshape(experts, GROUP, slots, width), axis=1).astype(jnp.bfloat16)
    mixed = jnp.dot(
        combine,
        summed.reshape(experts * slots, width).astype(jnp.float32),
        precision=lax.Precision.HIGHEST,
    )
    return mixed.astype(jnp.bfloat16)


CORE, X, Y, Z = 1, 2, 4, 8
COUNT = PLANES * GROUP


def swap(value, bits):
    return lax.ppermute(value, "node", [(i, i ^ bits) for i in range(COUNT)])


VMEM = 56 * 2**20


def shift(value, by, planes):
    moves = ((1, 0), (2, 3)) if by is None else [(p, p + by) for p in planes]
    return lax.ppermute(
        value,
        "node",
        [(p * GROUP + m, q * GROUP + m) for p, q in moves for m in range(GROUP)],
    )


def swiglu_kernel(own, by_x, by_y, low, high, gate_a, gate_b, up_a, up_b, out, gate, up):
    step = pl.program_id(0)

    @pl.when(step == 0)
    def _():
        gate[...] = jnp.zeros_like(gate)
        up[...] = jnp.zeros_like(up)

    block = jnp.concatenate([own[...], by_x[...], by_y[...], low[...], high[...]], axis=0)
    gate_w = jnp.concatenate([gate_a[...], gate_b[...]], axis=1)
    up_w = jnp.concatenate([up_a[...], up_b[...]], axis=1)
    gate[...] += jnp.dot(block, gate_w, preferred_element_type=jnp.float32)
    up[...] += jnp.dot(block, up_w, preferred_element_type=jnp.float32)

    @pl.when(step == pl.num_programs(0) - 1)
    def _():
        out[...] = (jax.nn.silu(gate[...]) * up[...]).astype(out.dtype)


def swiglu(pieces, weights):
    rows = sum(n for p, n, place in pieces)
    width = pieces[0][0].shape[1]
    hidden = sum(w.shape[1] for w in weights) // 2
    depth = width // 7
    return pl.pallas_call(
        swiglu_kernel,
        out_shape=jax.ShapeDtypeStruct((rows, hidden), jnp.bfloat16),
        grid=(7,),
        in_specs=[
            pl.BlockSpec((n, depth), lambda i, place=place: (place, i))
            for p, n, place in pieces
        ]
        + [pl.BlockSpec((depth, w.shape[1]), lambda i: (i, 0)) for w in weights],
        out_specs=pl.BlockSpec((rows, hidden), lambda i: (0, 0)),
        scratch_shapes=[pltpu.VMEM((rows, hidden), jnp.float32)] * 2,
        compiler_params=pltpu.CompilerParams(vmem_limit_bytes=VMEM),
        cost_estimate=pl.CostEstimate(flops=1000, bytes_accessed=1000, transcendentals=0),
    )(*[p for p, n, place in pieces], *weights)


def down_kernel(own, by_x, by_y, across, mine, other, out, hidden):
    rows = own.shape[0] // 4
    half = own.shape[1] // 2

    @pl.when(pl.program_id(0) == 0)
    def _():
        for r, unit in enumerate((own, by_x, by_y, across)):
            for j in range(4):
                block = unit[(j ^ r) * rows : (j ^ r) * rows + rows]
                for h in range(2):
                    hidden[
                        j * rows : j * rows + rows, (h * 4 + r) * half : (h * 4 + r + 1) * half
                    ] = block[:, h * half : (h + 1) * half]

    total = jnp.dot(hidden[:, : 4 * half], mine[...], preferred_element_type=jnp.float32)
    total += jnp.dot(hidden[:, 4 * half :], other[...], preferred_element_type=jnp.float32)
    out[...] = total.astype(out.dtype)


def down(pieces, weights):
    rows, hidden = pieces[0].shape
    width = weights[0].shape[1]
    cols = width // 2
    return pl.pallas_call(
        down_kernel,
        out_shape=jax.ShapeDtypeStruct((rows, width), jnp.bfloat16),
        grid=(2,),
        in_specs=[pl.BlockSpec(p.shape, lambda i: (0, 0)) for p in pieces]
        + [pl.BlockSpec((w.shape[0], cols), lambda i: (0, i)) for w in weights],
        out_specs=pl.BlockSpec((rows, cols), lambda i: (0, i)),
        scratch_shapes=[pltpu.VMEM((rows, 4 * hidden), jnp.bfloat16)],
        compiler_params=pltpu.CompilerParams(vmem_limit_bytes=VMEM),
        cost_estimate=pl.CostEstimate(
            flops=1000,
            bytes_accessed=1000,
            transcendentals=0,
        ),
    )(*pieces, *weights)


def nothing(*refs):
    pass


def after(values, *earlier):
    values = tuple(values)
    return pl.pallas_call(
        nothing,
        out_shape=[jax.ShapeDtypeStruct(v.shape, v.dtype) for v in values],
        in_specs=[pl.BlockSpec(memory_space=pl.ANY)] * (len(values) + len(earlier)),
        out_specs=[pl.BlockSpec(memory_space=pl.ANY)] * len(values),
        input_output_aliases={i: i for i in range(len(values))},
        compiler_params=pltpu.CompilerParams(vmem_limit_bytes=2**20),
        cost_estimate=pl.CostEstimate(flops=0, bytes_accessed=0, transcendentals=0),
    )(*values, *earlier)


def four_planes(tokens, routes, probs, w_gate, w_up, w_down):
    rows, width = tokens.shape
    part = width // 4
    half = rows // 2
    me = lax.axis_index("node")
    z = me // GROUP
    quarter = me // 2 % 4
    chain = [jnp.zeros((8, 128), jnp.float32)]

    def gate(values, *earlier):
        chain[0], *values = after([chain[0], *values], *earlier)
        return values

    def cut(r):
        return lax.dynamic_slice_in_dim(w_down[0], (quarter ^ r) * part, part, axis=1)

    experts = jnp.arange(PLANES, dtype=jnp.int32)
    weights = jnp.sum(
        jnp.where(routes[:, :, None] == experts, probs[:, :, None], 0.0), axis=1
    )

    up1, dn1 = shift(tokens, 1, (0, 1, 2)), shift(tokens, -1, (1, 2, 3))
    down_x, down_y = swap(cut(1), X), swap(cut(2), Y)
    gate_b, up_b = swap(w_gate[0], CORE), swap(w_up[0], CORE)

    up1, dn1, piece = gate([up1, dn1, cut(3)], down_x, down_y)
    up2, dn2, down_d = shift(up1, 1, (1, 2)), shift(dn1, -1, (1, 2)), swap(piece, X + Y)

    col = {0: tokens, 1: jnp.where(z % 2 == 0, dn1, up1), 2: jnp.where(z < 2, dn2, up2)}
    onward = jnp.where(z == 2, up2, dn2)
    mx, onward, down_x = gate([col[2], onward, down_x], down_d, gate_b)
    col[2] = mx
    x2, y2 = swap(mx, X), swap(mx, Y)
    ends = shift(onward, None, None)
    down_mine = jnp.concatenate([cut(0), down_x, down_y, down_d], axis=0)
    down_w = [down_mine, swap(down_mine, CORE)]
    col[3] = jnp.where((z == 0) | (z == 3), ends, jnp.where(z == 1, dn1, up1))
    swiglu_w = [w_gate[0], gate_b, w_up[0], up_b]

    def join(ahead, by_x, by_y):
        low, high = by_x[:half], by_y[half:rows]
        if ahead is None:
            return high, low
        return jnp.concatenate([ahead, high], axis=0), jnp.concatenate([ahead, low], axis=0)

    def rows_of(k, by_x, by_y, by_x_later, by_y_later):
        place = (by_x_later.shape[0] - half) // half
        return [(col[k], rows, 0), (by_x, rows, 0), (by_y, rows, 0)] + [
            (by_y_later, half, place),
            (by_x_later, half, place),
        ]

    def spread(hidden):
        (hidden,) = gate([hidden])
        return [hidden, swap(hidden, X), swap(hidden, Y), swap(hidden, X + Y)]

    def send_back(units, k):
        (units[0],) = gate([units[0]])
        out = down(units, down_w)
        low, high = gate([out[: 2 * rows], out[2 * rows :]])
        return swap(low, k * Z), swap(high, k * Z)

    sums = {}
    mx, my, w_0 = gate([*join(col[3], x2, y2), weights], down_w[1], up_b)
    x3, y3 = swap(mx, X), swap(my, Y)
    w_x, w_y, w_d = swap(w_0, X), swap(w_0, Y), swap(w_0, X + Y)

    mx, my = gate(join(col[1], x3, y3), w_x, w_y, w_d)
    x1, y1 = swap(mx, X), swap(my, Y)
    (mark,) = gate([x2])
    all_2 = spread(swiglu(rows_of(2, mark, y2, x3, y3), swiglu_w))

    mx, my, all_2[0] = gate([*join(tokens, x1, y1), all_2[0]], *all_2[1:])
    x0, y0 = swap(mx, X), swap(my, Y)
    sums[2] = send_back(all_2, 2)
    (mark,) = gate([x3])
    all_3 = spread(swiglu(rows_of(3, mark, y3, x1, y1), swiglu_w))

    mx, my, all_3[0] = gate([*join(None, x0, y0), all_3[0]], sums[2][0], *all_3[1:])
    xe, ye = swap(mx, X), swap(my, Y)
    sums[3] = send_back(all_3, 3)
    (mark,) = gate([x1])
    all_1 = spread(swiglu(rows_of(1, mark, y1, x0, y0), swiglu_w))

    (ye,) = gate([ye], xe, sums[2][1], sums[3][0], *all_1[1:])
    all_0 = spread(swiglu(rows_of(0, x0, y0, xe, ye), swiglu_w))
    sums[1] = send_back(all_1, 1)
    (all_0[0],) = gate([all_0[0]], *all_0[1:])
    sums[0] = (down(all_0, down_w),)
    order = (2, 3, 1, 0)
    sums = {k: jnp.concatenate(sums[k], axis=0) for k in order}

    weights = jnp.concatenate([w_0, w_x, w_y, w_d], axis=0)
    total = 0.0
    for k in order:
        weight = jnp.sum(jnp.where(experts == (z ^ k), weights, 0.0), axis=1, keepdims=True)
        total = total + weight * sums[k].astype(jnp.float32)
    mixed = total.astype(jnp.bfloat16).reshape(4, rows, part)
    pieces = [mixed[0], swap(mixed[1], X), swap(mixed[2], Y), swap(mixed[3], X + Y)]
    result = []
    for a in range(4):
        piece = pieces[a]
        for q in range(1, 4):
            piece = jnp.where(quarter == q, pieces[a ^ q], piece)
        result.append(piece)
    return jnp.concatenate(result, axis=1)


def solution(mesh):
    devices = mesh.shape["node"]

    def per_device(tokens, routes, probs, w_gate, w_up, w_down):
        path = four_planes if devices == COUNT else general
        return path(tokens, routes, probs, w_gate, w_up, w_down)

    in_specs = (
        P(("rep", "node"), None),
        P(("rep", "node"), None),
        P(("rep", "node"), None),
        P("node", None, None),
        P("node", None, None),
        P("node", None, None),
    )
    out_specs = P(("rep", "node"), None)
    return jax.shard_map(
        per_device, mesh=mesh, in_specs=in_specs, out_specs=out_specs, check_vma=False
    )
```

```python
import jax
import jax.numpy as jnp
from jax import lax
from jax.experimental import pallas as pl
from jax.experimental.pallas import tpu as pltpu
from jax.sharding import PartitionSpec as P

GROUP = 8
PLANES = 4


def general(tokens, routes, probs, w_gate, w_up, w_down):
    tok_rows, width = tokens.shape
    chosen_count = routes.shape[1]
    devices = lax.axis_size("node")
    experts = devices // GROUP
    slots = min(tok_rows, GROUP * max(1, 2 * tok_rows * chosen_count // (experts * GROUP)))
    flat_routes = routes.reshape(-1)
    onehot = (flat_routes[:, None] == jnp.arange(experts, dtype=jnp.int32)[None, :]).astype(
        jnp.int32
    )
    ranks = jnp.sum((jnp.cumsum(onehot, axis=0) - onehot) * onehot, axis=1)
    target = flat_routes * slots + ranks
    placed = target[:, None] == jnp.arange(experts * slots, dtype=jnp.int32)[None, :]
    placed = placed.reshape(tok_rows, chosen_count, experts * slots)
    sender = jnp.sum(placed.astype(jnp.float32), axis=1).astype(jnp.bfloat16)
    combine = jnp.sum(jnp.where(placed, probs[:, :, None], 0.0), axis=1)
    packed = lax.dot_general(
        sender, tokens, (((0,), (0,)), ((), ())), preferred_element_type=jnp.float32
    ).astype(jnp.bfloat16)
    spread = jnp.broadcast_to(
        packed.reshape(experts, 1, slots, width), (experts, GROUP, slots, width)
    )
    spread = spread.reshape(devices, slots, width)
    block = lax.all_to_all(spread, "node", split_axis=0, concat_axis=0, tiled=True)
    lead = block.shape[:-1]
    flat_rows = block.reshape(-1, width)
    gate = jnp.dot(flat_rows, w_gate[0], preferred_element_type=jnp.float32)
    up = jnp.dot(flat_rows, w_up[0], preferred_element_type=jnp.float32)
    hidden = (jax.nn.silu(gate) * up).astype(jnp.bfloat16)
    returned = lax.all_to_all(
        jnp.dot(hidden, w_down[0], preferred_element_type=jnp.float32).reshape(lead + (width,)),
        "node",
        split_axis=0,
        concat_axis=0,
        tiled=True,
    )
    summed = jnp.sum(returned.reshape(experts, GROUP, slots, width), axis=1).astype(jnp.bfloat16)
    mixed = jnp.dot(
        combine,
        summed.reshape(experts * slots, width).astype(jnp.float32),
        precision=lax.Precision.HIGHEST,
    )
    return mixed.astype(jnp.bfloat16)


CORE, X, Y, Z = 1, 2, 4, 8
COUNT = PLANES * GROUP


def swap(value, bits):
    return lax.ppermute(value, "node", [(i, i ^ bits) for i in range(COUNT)])


VMEM = 16 * 2**20


def shift(value, by, planes):
    moves = ((1, 0), (2, 3)) if by is None else [(p, p + by) for p in planes]
    return lax.ppermute(
        value,
        "node",
        [(p * GROUP + m, q * GROUP + m) for p, q in moves for m in range(GROUP)],
    )


def swiglu_kernel(*refs):
    *pieces, gate_a, gate_b, up_a, up_b, out, gate, up = refs
    step = pl.program_id(0)

    @pl.when(step == 0)
    def _():
        gate[...] = jnp.zeros_like(gate)
        up[...] = jnp.zeros_like(up)

    block = jnp.concatenate([p[...] for p in pieces], axis=0)
    gate_w = jnp.concatenate([gate_a[...], gate_b[...]], axis=1)
    up_w = jnp.concatenate([up_a[...], up_b[...]], axis=1)
    gate[...] += jnp.dot(block, gate_w, preferred_element_type=jnp.float32)
    up[...] += jnp.dot(block, up_w, preferred_element_type=jnp.float32)

    @pl.when(step == pl.num_programs(0) - 1)
    def _():
        out[...] = (jax.nn.silu(gate[...]) * up[...]).astype(out.dtype)


def swiglu(pieces, weights):
    rows = sum(n for p, n, place in pieces)
    width = pieces[0][0].shape[1]
    hidden = sum(w.shape[1] for w in weights) // 2
    depth = width // 7
    return pl.pallas_call(
        swiglu_kernel,
        out_shape=jax.ShapeDtypeStruct((rows, hidden), jnp.bfloat16),
        grid=(7,),
        in_specs=[
            pl.BlockSpec((n, depth), lambda i, place=place: (place, i))
            for p, n, place in pieces
        ]
        + [pl.BlockSpec((depth, w.shape[1]), lambda i: (i, 0)) for w in weights],
        out_specs=pl.BlockSpec((rows, hidden), lambda i: (0, 0)),
        scratch_shapes=[pltpu.VMEM((rows, hidden), jnp.float32)] * 2,
        compiler_params=pltpu.CompilerParams(vmem_limit_bytes=VMEM),
        cost_estimate=pl.CostEstimate(flops=1000, bytes_accessed=1000, transcendentals=0),
    )(*[p for p, n, place in pieces], *weights)


def down_kernel(own, by_x, by_y, across, mine, other, *rest):
    *mix, out, hidden = rest
    rows = own.shape[0] // 4
    half = own.shape[1] // 2

    @pl.when(pl.program_id(0) == 0)
    def _():
        for r, unit in enumerate((own, by_x, by_y, across)):
            for j in range(4):
                block = unit[(j ^ r) * rows : (j ^ r) * rows + rows]
                for h in range(2):
                    hidden[
                        j * rows : j * rows + rows, (h * 4 + r) * half : (h * 4 + r + 1) * half
                    ] = block[:, h * half : (h + 1) * half]

    total = jnp.dot(hidden[:, : 4 * half], mine[...], preferred_element_type=jnp.float32)
    total += jnp.dot(hidden[:, 4 * half :], other[...], preferred_element_type=jnp.float32)
    total = total.astype(out.dtype)
    if mix:
        weights, *others = mix
        total = weights[:, 0:1] * total.astype(jnp.float32)
        for k, term in enumerate(others, 1):
            total += weights[:, k : k + 1] * term[...].astype(jnp.float32)
    out[...] = total.astype(out.dtype)


def down(pieces, weights, mix=()):
    rows, hidden = pieces[0].shape
    width = weights[0].shape[1]
    cols = width // 2
    return pl.pallas_call(
        down_kernel,
        out_shape=jax.ShapeDtypeStruct((rows, width), jnp.bfloat16),
        grid=(2,),
        in_specs=[pl.BlockSpec(p.shape, lambda i: (0, 0)) for p in pieces]
        + [pl.BlockSpec((w.shape[0], cols), lambda i: (0, i)) for w in weights]
        + [pl.BlockSpec(m.shape, lambda i: (0, 0)) for m in mix[:1]]
        + [pl.BlockSpec((rows, cols), lambda i: (0, i)) for m in mix[1:]],
        out_specs=pl.BlockSpec((rows, cols), lambda i: (0, i)),
        scratch_shapes=[pltpu.VMEM((rows, 4 * hidden), jnp.bfloat16)],
        compiler_params=pltpu.CompilerParams(vmem_limit_bytes=56 * 2**20 if mix else VMEM),
        cost_estimate=pl.CostEstimate(flops=1000, bytes_accessed=1000, transcendentals=0),
    )(*pieces, *weights, *mix)


def nothing(*refs):
    pass


def after(values, *earlier):
    values = tuple(values)
    return pl.pallas_call(
        nothing,
        out_shape=[jax.ShapeDtypeStruct(v.shape, v.dtype) for v in values],
        in_specs=[pl.BlockSpec(memory_space=pl.ANY)] * (len(values) + len(earlier)),
        out_specs=[pl.BlockSpec(memory_space=pl.ANY)] * len(values),
        input_output_aliases={i: i for i in range(len(values))},
        compiler_params=pltpu.CompilerParams(vmem_limit_bytes=2**20),
        cost_estimate=pl.CostEstimate(flops=0, bytes_accessed=0, transcendentals=0),
    )(*values, *earlier)


def four_planes(tokens, routes, probs, w_gate, w_up, w_down):
    rows, width = tokens.shape
    part = width // 4
    half = rows // 2
    me = lax.axis_index("node")
    z = me // GROUP
    quarter = me // 2 % 4
    chain = [jnp.zeros((8, 128), jnp.float32)]

    def gate(values, *earlier):
        chain[0], *values = after([chain[0], *values], *earlier)
        return values

    def cut(r):
        return lax.dynamic_slice_in_dim(w_down[0], (quarter ^ r) * part, part, axis=1)

    experts = jnp.arange(PLANES, dtype=jnp.int32)
    weights = jnp.sum(
        jnp.where(routes[:, :, None] == experts, probs[:, :, None], 0.0), axis=1
    )

    def join(*pieces):
        return jnp.concatenate(pieces, axis=0)

    def spread(hidden):
        (hidden,) = gate([hidden])
        return [hidden, swap(hidden, X), swap(hidden, Y), swap(hidden, X + Y)]

    def outputs(units, *earlier):
        (units[0],) = gate([units[0]], *earlier)
        out = down(units, down_w)
        return gate([out])

    up1, dn1 = shift(tokens, 1, (0, 1, 2)), shift(tokens, -1, (1, 2, 3))
    down_x, down_y = swap(cut(1), X), swap(cut(2), Y)
    gate_b, up_b = swap(w_gate[0], CORE), swap(w_up[0], CORE)
    up1, dn1 = gate([up1, dn1])
    up2, dn2 = shift(up1, 1, (1, 2)), shift(dn1, -1, (1, 2))
    (piece,) = gate([cut(3)], down_x, down_y)
    down_d = swap(piece, X + Y)
    (onward,) = gate([jnp.where(z == 2, up2, dn2)])
    ends = shift(onward, None, None)

    col1 = jnp.where(z % 2 == 0, dn1, up1)
    col2 = jnp.where(z < 2, dn2, up2)
    col2, down_x, w_0 = gate([col2, down_x, weights], down_y, down_d)
    x2, y2 = swap(col2, X), swap(col2, Y)
    w_x = swap(w_0, X)
    down_mine = jnp.concatenate([cut(0), down_x, down_y, down_d], axis=0)
    down_w = [down_mine, swap(down_mine, CORE)]
    swiglu_w = [w_gate[0], gate_b, w_up[0], up_b]

    col3 = jnp.where((z == 0) | (z == 3), ends, jnp.where(z == 1, dn1, up1))
    to_x, to_y, to_z, w_0 = gate(
        [
            join(col3[half:], y2[half:]),
            join(col3[:half], x2[:half]),
            join(x2[:half], y2[half:]),
            w_0,
        ],
        down_w[1],
        gate_b,
        w_x,
    )
    x3, y3, z3 = swap(to_x, X), swap(to_y, Y), swap(to_z, Z)
    w_y = swap(w_0, Y)

    col1, to_z, w_0 = gate([col1, join(y3[half:], x3[half:]), w_0], z3, up_b, w_y)
    x1, y1, d3 = swap(col1, X), swap(col1, Y), swap(to_z, Z)
    w_d = swap(w_0, X + Y)
    (mark,) = gate([x2])
    all_2 = spread(
        swiglu(
            [(col2, rows, 0), (mark, rows, 0), (y2, rows, 0), (y3, half, 1), (x3, half, 1)],
            swiglu_w,
        )
    )

    to_x, to_y, all_2[0] = gate([y1[half:], x1[:half], all_2[0]], d3, w_d, *all_2[1:])
    high1, low1 = swap(to_x, X), swap(to_y, Y)
    (out_2,) = outputs(all_2)
    back_2 = [swap(out_2, 2 * Z)]
    (own,) = gate([tokens], low1, high1)
    x0, y0 = swap(own, X), swap(own, Y)
    (mark,) = gate([col3])
    all_3 = spread(
        swiglu(
            [
                (mark, rows, 0),
                (z3, half, 0),
                (x3, half, 0),
                (y3, half, 0),
                (z3, half, 1),
                (d3, rows, 0),
            ],
            swiglu_w,
        )
    )
    (mark,) = gate([col1])
    hidden_1 = swiglu(
        [(mark, rows, 0), (x1, rows, 0), (y1, rows, 0), (low1, half, 0), (high1, half, 0)],
        swiglu_w,
    )

    to_x, to_y, all_3[0], hidden_1 = gate(
        [y0[half:], x0[:half], all_3[0], hidden_1], *all_3[1:]
    )
    xe, ye = swap(to_x, X), swap(to_y, Y)
    (hidden_1,) = gate([hidden_1])
    all_1 = [hidden_1, swap(hidden_1, X), swap(hidden_1, Y)]
    (out_3,) = outputs(all_3)
    back_3 = [swap(out_3, 3 * Z)]
    xe, all_1[0] = gate([xe, all_1[0]], ye, *back_2)
    all_1.append(swap(all_1[0], X + Y))
    all_0 = spread(
        swiglu(
            [(own, rows, 0), (x0, rows, 0), (y0, rows, 0), (ye, half, 0), (xe, half, 0)],
            swiglu_w,
        )
    )
    (out_1,) = outputs(all_1, *all_1[1:])
    back_1 = [swap(out_1, Z)]
    (all_0[0],) = gate([all_0[0]], *all_0[1:])
    weights = jnp.concatenate([w_0, w_x, w_y, w_d], axis=0)
    weights = jnp.concatenate(
        [
            jnp.sum(jnp.where(experts == (z ^ k), weights, 0.0), axis=1, keepdims=True)
            for k in range(PLANES)
        ],
        axis=1,
    )
    mixed = down(all_0, down_w, [weights, back_1[0], back_2[0], back_3[0]]).reshape(4, rows, part)
    pieces = [mixed[0], swap(mixed[1], X), swap(mixed[2], Y), swap(mixed[3], X + Y)]
    result = []
    for a in range(4):
        piece = pieces[a]
        for q in range(1, 4):
            piece = jnp.where(quarter == q, pieces[a ^ q], piece)
        result.append(piece)
    return jnp.concatenate(result, axis=1)


def solution(mesh):
    devices = mesh.shape["node"]

    def per_device(tokens, routes, probs, w_gate, w_up, w_down):
        path = four_planes if devices == COUNT else general
        return path(tokens, routes, probs, w_gate, w_up, w_down)

    in_specs = (
        P(("rep", "node"), None),
        P(("rep", "node"), None),
        P(("rep", "node"), None),
        P("node", None, None),
        P("node", None, None),
        P("node", None, None),
    )
    out_specs = P(("rep", "node"), None)
    return jax.shard_map(
        per_device, mesh=mesh, in_specs=in_specs, out_specs=out_specs, check_vma=False
    )
```

```python
import jax
import jax.numpy as jnp
from jax import lax
from jax.experimental import pallas as pl
from jax.experimental.pallas import tpu as pltpu
from jax.sharding import PartitionSpec as P

GROUP = 8
PLANES = 4


def general(tokens, routes, probs, w_gate, w_up, w_down):
    tok_rows, width = tokens.shape
    chosen_count = routes.shape[1]
    devices = lax.axis_size("node")
    experts = devices // GROUP
    slots = min(tok_rows, GROUP * max(1, 2 * tok_rows * chosen_count // (experts * GROUP)))
    flat_routes = routes.reshape(-1)
    onehot = (flat_routes[:, None] == jnp.arange(experts, dtype=jnp.int32)[None, :]).astype(
        jnp.int32
    )
    ranks = jnp.sum((jnp.cumsum(onehot, axis=0) - onehot) * onehot, axis=1)
    target = flat_routes * slots + ranks
    placed = target[:, None] == jnp.arange(experts * slots, dtype=jnp.int32)[None, :]
    placed = placed.reshape(tok_rows, chosen_count, experts * slots)
    sender = jnp.sum(placed.astype(jnp.float32), axis=1).astype(jnp.bfloat16)
    combine = jnp.sum(jnp.where(placed, probs[:, :, None], 0.0), axis=1)
    packed = lax.dot_general(
        sender, tokens, (((0,), (0,)), ((), ())), preferred_element_type=jnp.float32
    ).astype(jnp.bfloat16)
    spread = jnp.broadcast_to(
        packed.reshape(experts, 1, slots, width), (experts, GROUP, slots, width)
    )
    spread = spread.reshape(devices, slots, width)
    block = lax.all_to_all(spread, "node", split_axis=0, concat_axis=0, tiled=True)
    lead = block.shape[:-1]
    flat_rows = block.reshape(-1, width)
    gate = jnp.dot(flat_rows, w_gate[0], preferred_element_type=jnp.float32)
    up = jnp.dot(flat_rows, w_up[0], preferred_element_type=jnp.float32)
    hidden = (jax.nn.silu(gate) * up).astype(jnp.bfloat16)
    returned = lax.all_to_all(
        jnp.dot(hidden, w_down[0], preferred_element_type=jnp.float32).reshape(lead + (width,)),
        "node",
        split_axis=0,
        concat_axis=0,
        tiled=True,
    )
    summed = jnp.sum(returned.reshape(experts, GROUP, slots, width), axis=1).astype(jnp.bfloat16)
    mixed = jnp.dot(
        combine,
        summed.reshape(experts * slots, width).astype(jnp.float32),
        precision=lax.Precision.HIGHEST,
    )
    return mixed.astype(jnp.bfloat16)


CORE, X, Y, Z = 1, 2, 4, 8
COUNT = PLANES * GROUP


def swap(value, bits):
    return lax.ppermute(value, "node", [(i, i ^ bits) for i in range(COUNT)])


VMEM = 16 * 2**20


def swiglu_kernel(*refs):
    *pieces, gate_a, gate_b, up_a, up_b, out, gate, up = refs
    step = pl.program_id(0)

    @pl.when(step == 0)
    def _():
        gate[...] = jnp.zeros_like(gate)
        up[...] = jnp.zeros_like(up)

    block = jnp.concatenate([p[...] for p in pieces], axis=0)
    gate_w = jnp.concatenate([gate_a[...], gate_b[...]], axis=1)
    up_w = jnp.concatenate([up_a[...], up_b[...]], axis=1)
    gate[...] += jnp.dot(block, gate_w, preferred_element_type=jnp.float32)
    up[...] += jnp.dot(block, up_w, preferred_element_type=jnp.float32)

    @pl.when(step == pl.num_programs(0) - 1)
    def _():
        out[...] = (jax.nn.silu(gate[...]) * up[...]).astype(out.dtype)


def swiglu(pieces, weights):
    rows = sum(n for p, n, place in pieces)
    width = pieces[0][0].shape[1]
    hidden = sum(w.shape[1] for w in weights) // 2
    depth = width // 7
    return pl.pallas_call(
        swiglu_kernel,
        out_shape=jax.ShapeDtypeStruct((rows, hidden), jnp.bfloat16),
        grid=(7,),
        in_specs=[
            pl.BlockSpec((n, depth), lambda i, place=place: (place, i))
            for p, n, place in pieces
        ]
        + [pl.BlockSpec((depth, w.shape[1]), lambda i: (i, 0)) for w in weights],
        out_specs=pl.BlockSpec((rows, hidden), lambda i: (0, 0)),
        scratch_shapes=[pltpu.VMEM((rows, hidden), jnp.float32)] * 2,
        compiler_params=pltpu.CompilerParams(vmem_limit_bytes=VMEM),
        cost_estimate=pl.CostEstimate(flops=1000, bytes_accessed=1000, transcendentals=0),
    )(*[p for p, n, place in pieces], *weights)


def down_kernel(own, by_x, by_y, across, mine, other, *rest):
    *mix, out, hidden = rest
    rows = own.shape[0] // 4
    half = own.shape[1] // 2

    @pl.when(pl.program_id(0) == 0)
    def _():
        for r, unit in enumerate((own, by_x, by_y, across)):
            for j in range(4):
                block = unit[(j ^ r) * rows : (j ^ r) * rows + rows]
                for h in range(2):
                    hidden[
                        j * rows : j * rows + rows, (h * 4 + r) * half : (h * 4 + r + 1) * half
                    ] = block[:, h * half : (h + 1) * half]

    total = jnp.dot(hidden[:, : 4 * half], mine[...], preferred_element_type=jnp.float32)
    total += jnp.dot(hidden[:, 4 * half :], other[...], preferred_element_type=jnp.float32)
    total = total.astype(out.dtype)
    if mix:
        weights, *others = mix
        total = weights[:, 0:1] * total.astype(jnp.float32)
        for k, term in enumerate(others, 1):
            total += weights[:, k : k + 1] * term[...].astype(jnp.float32)
    out[...] = total.astype(out.dtype)


def down(pieces, weights, mix=()):
    rows, hidden = pieces[0].shape
    width = weights[0].shape[1]
    cols = width // 2
    return pl.pallas_call(
        down_kernel,
        out_shape=jax.ShapeDtypeStruct((rows, width), jnp.bfloat16),
        grid=(2,),
        in_specs=[pl.BlockSpec(p.shape, lambda i: (0, 0)) for p in pieces]
        + [pl.BlockSpec((w.shape[0], cols), lambda i: (0, i)) for w in weights]
        + [pl.BlockSpec(m.shape, lambda i: (0, 0)) for m in mix[:1]]
        + [pl.BlockSpec((rows, cols), lambda i: (0, i)) for m in mix[1:]],
        out_specs=pl.BlockSpec((rows, cols), lambda i: (0, i)),
        scratch_shapes=[pltpu.VMEM((rows, 4 * hidden), jnp.bfloat16)],
        compiler_params=pltpu.CompilerParams(vmem_limit_bytes=56 * 2**20 if mix else VMEM),
        cost_estimate=pl.CostEstimate(flops=1000, bytes_accessed=1000, transcendentals=0),
    )(*pieces, *weights, *mix)


def nothing(*refs):
    pass


def after(values, *earlier):
    values = tuple(values)
    return pl.pallas_call(
        nothing,
        out_shape=[jax.ShapeDtypeStruct(v.shape, v.dtype) for v in values],
        in_specs=[pl.BlockSpec(memory_space=pl.ANY)] * (len(values) + len(earlier)),
        out_specs=[pl.BlockSpec(memory_space=pl.ANY)] * len(values),
        input_output_aliases={i: i for i in range(len(values))},
        compiler_params=pltpu.CompilerParams(vmem_limit_bytes=2**20),
        cost_estimate=pl.CostEstimate(flops=0, bytes_accessed=0, transcendentals=0),
    )(*values, *earlier)


def four_planes(tokens, routes, probs, w_gate, w_up, w_down):
    rows, width = tokens.shape
    part = width // 4
    half = rows // 2
    me = lax.axis_index("node")
    z = me // GROUP
    quarter = me // 2 % 4
    chain = [jnp.zeros((8, 128), jnp.float32)]

    def gate(values, *earlier):
        chain[0], *values = after([chain[0], *values], *earlier)
        return values

    def cut(r):
        return lax.dynamic_slice_in_dim(w_down[0], (quarter ^ r) * part, part, axis=1)

    experts = jnp.arange(PLANES, dtype=jnp.int32)
    weights = jnp.sum(
        jnp.where(routes[:, :, None] == experts, probs[:, :, None], 0.0), axis=1
    )

    def join(*pieces):
        return jnp.concatenate(pieces, axis=0)

    def spread(hidden, *earlier):
        (hidden,) = gate([hidden], *earlier)
        return [hidden, swap(hidden, X), swap(hidden, Y), swap(hidden, X + Y)]

    def outputs(units, *earlier, split=False):
        (units[0],) = gate([units[0]], *earlier)
        out = down(units, down_w)
        return gate([out[: 2 * rows], out[2 * rows :]] if split else [out])

    col2, col1 = swap(tokens, 2 * Z), swap(tokens, Z)
    down_x, down_y, down_d = swap(cut(1), X), swap(cut(2), Y), swap(cut(3), X + Y)

    col2, down_x = gate([col2, down_x], col1, down_y, down_d)
    gate_a, up_a = gate([w_gate[0], w_up[0]])
    x2, y2, col3 = swap(col2, X), swap(col2, Y), swap(col2, Z)
    gate_b, up_b = swap(gate_a, CORE), swap(up_a, CORE)
    down_mine = jnp.concatenate([cut(0), down_x, down_y, down_d], axis=0)

    to_x, to_y, to_z, down_mine, w_0 = gate(
        [y2[half:], x2[:half], x2[:half], down_mine, weights], col3, gate_b, up_b
    )
    high2, low2, z_x_low = swap(to_x, X), swap(to_y, Y), swap(to_z, Z)
    down_w = [down_mine, swap(down_mine, CORE)]
    w_x = swap(w_0, X)
    swiglu_w = [w_gate[0], gate_b, w_up[0], up_b]

    col1, low2, w_0, to_z = gate(
        [col1, low2, w_0, x2[half:]], high2, down_w[1], w_x, z_x_low
    )
    x1, y1, z_x_high = swap(col1, X), swap(col1, Y), swap(to_z, Z)
    hidden_2 = swiglu(
        [(col2, rows, 0), (x2, rows, 0), (y2, rows, 0), (low2, half, 0), (high2, half, 0)],
        swiglu_w,
    )
    hidden_2, y2 = gate([hidden_2, y2], z_x_high)
    all_2 = [hidden_2, swap(hidden_2, X), swap(hidden_2, Y)]
    z_y = swap(y2, Z)
    x1, all_2[0] = gate([x1, all_2[0]], y1)
    all_2.append(swap(all_2[0], X + Y))

    to_x, to_y, to_z, all_2[0], w_0 = gate(
        [
            join(y1[half:], tokens[:half]),
            join(x1[:half], tokens[half:]),
            join(low2, high2),
            all_2[0],
            w_0,
        ],
        z_y,
        *all_2[1:],
    )
    x4, y4, zb = swap(to_x, X), swap(to_y, Y), swap(to_z, Z)
    w_y = swap(w_0, Y)
    first, second = outputs(all_2, split=True)
    back_2 = [swap(first, 2 * Z)]

    to_x, to_y, second, w_0 = gate(
        [tokens[half:], tokens[:half], second, w_0], zb, x4, y4, w_y
    )
    x5, y5 = swap(to_x, X), swap(to_y, Y)
    back_2.append(swap(second, 2 * Z))
    w_d = swap(w_0, X + Y)
    (mark,) = gate([col3])
    all_3 = spread(
        swiglu(
            [
                (mark, rows, 0),
                (z_x_low, half, 0),
                (z_x_high, half, 0),
                (z_y, rows, 0),
                (zb, rows, 0),
            ],
            swiglu_w,
        ),
        x5,
        y5,
        back_2[0],
    )
    (mark,) = gate([col1])
    hidden_1 = swiglu(
        [(mark, rows, 0), (x1, rows, 0), (y1, rows, 0), (y4, half, 0), (x4, half, 0)], swiglu_w
    )

    to_x, to_y, all_3[0], hidden_1 = gate(
        [y4[half:], x4[half:], all_3[0], hidden_1], w_d, back_2[1], *all_3[1:]
    )
    xe, ye = swap(to_x, X), swap(to_y, Y)
    (out_3,) = outputs(all_3)
    back_3 = [swap(out_3, 3 * Z)]
    (hidden_1,) = gate([hidden_1])
    all_1 = [hidden_1, swap(hidden_1, X), swap(hidden_1, Y)]

    xe, all_1[0] = gate([xe, all_1[0]], ye)
    all_1.append(swap(all_1[0], X + Y))
    all_0 = spread(
        swiglu(
            [
                (tokens, rows, 0),
                (x4, half, 1),
                (x5, half, 0),
                (y5, half, 0),
                (y4, half, 1),
                (ye, half, 0),
                (xe, half, 0),
            ],
            swiglu_w,
        )
    )
    (out_1,) = outputs(all_1, *all_1[1:])
    back_1 = [swap(out_1, Z)]
    (all_0[0],) = gate([all_0[0]], *all_0[1:])
    back_2 = [jnp.concatenate(back_2, axis=0)]
    weights = jnp.concatenate([w_0, w_x, w_y, w_d], axis=0)
    weights = jnp.concatenate(
        [
            jnp.sum(jnp.where(experts == (z ^ k), weights, 0.0), axis=1, keepdims=True)
            for k in range(PLANES)
        ],
        axis=1,
    )
    sums = [down(all_0, down_w), back_1[0], back_2[0], back_3[0]]
    total = sum(weights[:, k : k + 1] * sums[k].astype(jnp.float32) for k in range(PLANES))
    mixed = total.astype(jnp.bfloat16).reshape(4, rows, part)
    pieces = [mixed[0], swap(mixed[1], X), swap(mixed[2], Y), swap(mixed[3], X + Y)]
    result = []
    for a in range(4):
        piece = pieces[a]
        for q in range(1, 4):
            piece = jnp.where(quarter == q, pieces[a ^ q], piece)
        result.append(piece)
    return jnp.concatenate(result, axis=1)


def solution(mesh):
    devices = mesh.shape["node"]

    def per_device(tokens, routes, probs, w_gate, w_up, w_down):
        path = four_planes if devices == COUNT else general
        return path(tokens, routes, probs, w_gate, w_up, w_down)

    in_specs = (
        P(("rep", "node"), None),
        P(("rep", "node"), None),
        P(("rep", "node"), None),
        P("node", None, None),
        P("node", None, None),
        P("node", None, None),
    )
    out_specs = P(("rep", "node"), None)
    return jax.shard_map(
        per_device, mesh=mesh, in_specs=in_specs, out_specs=out_specs, check_vma=False
    )
```

```python
import jax
import jax.numpy as jnp
from jax import lax
from jax.experimental import pallas as pl
from jax.experimental.pallas import tpu as pltpu
from jax.sharding import PartitionSpec as P

GROUP = 8
PLANES = 4


def general(tokens, routes, probs, w_gate, w_up, w_down):
    tok_rows, width = tokens.shape
    chosen_count = routes.shape[1]
    devices = lax.axis_size("node")
    experts = devices // GROUP
    slots = min(tok_rows, GROUP * max(1, 2 * tok_rows * chosen_count // (experts * GROUP)))
    flat_routes = routes.reshape(-1)
    onehot = (flat_routes[:, None] == jnp.arange(experts, dtype=jnp.int32)[None, :]).astype(
        jnp.int32
    )
    ranks = jnp.sum((jnp.cumsum(onehot, axis=0) - onehot) * onehot, axis=1)
    target = flat_routes * slots + ranks
    placed = target[:, None] == jnp.arange(experts * slots, dtype=jnp.int32)[None, :]
    placed = placed.reshape(tok_rows, chosen_count, experts * slots)
    sender = jnp.sum(placed.astype(jnp.float32), axis=1).astype(jnp.bfloat16)
    combine = jnp.sum(jnp.where(placed, probs[:, :, None], 0.0), axis=1)
    packed = lax.dot_general(
        sender, tokens, (((0,), (0,)), ((), ())), preferred_element_type=jnp.float32
    ).astype(jnp.bfloat16)
    spread = jnp.broadcast_to(
        packed.reshape(experts, 1, slots, width), (experts, GROUP, slots, width)
    )
    spread = spread.reshape(devices, slots, width)
    block = lax.all_to_all(spread, "node", split_axis=0, concat_axis=0, tiled=True)
    lead = block.shape[:-1]
    flat_rows = block.reshape(-1, width)
    gate = jnp.dot(flat_rows, w_gate[0], preferred_element_type=jnp.float32)
    up = jnp.dot(flat_rows, w_up[0], preferred_element_type=jnp.float32)
    hidden = (jax.nn.silu(gate) * up).astype(jnp.bfloat16)
    returned = lax.all_to_all(
        jnp.dot(hidden, w_down[0], preferred_element_type=jnp.float32).reshape(lead + (width,)),
        "node",
        split_axis=0,
        concat_axis=0,
        tiled=True,
    )
    summed = jnp.sum(returned.reshape(experts, GROUP, slots, width), axis=1).astype(jnp.bfloat16)
    mixed = jnp.dot(
        combine,
        summed.reshape(experts * slots, width).astype(jnp.float32),
        precision=lax.Precision.HIGHEST,
    )
    return mixed.astype(jnp.bfloat16)


CORE, X, Y, Z = 1, 2, 4, 8
COUNT = PLANES * GROUP


def swap(value, bits):
    return lax.ppermute(value, "node", [(i, i ^ bits) for i in range(COUNT)])


VMEM = 16 * 2**20


def swiglu_kernel(*refs):
    *pieces, gate_a, gate_b, up_a, up_b, out, gate, up = refs
    step = pl.program_id(0)

    @pl.when(step == 0)
    def _():
        gate[...] = jnp.zeros_like(gate)
        up[...] = jnp.zeros_like(up)

    block = jnp.concatenate([p[...] for p in pieces], axis=0)
    gate_w = jnp.concatenate([gate_a[...], gate_b[...]], axis=1)
    up_w = jnp.concatenate([up_a[...], up_b[...]], axis=1)
    gate[...] += jnp.dot(block, gate_w, preferred_element_type=jnp.float32)
    up[...] += jnp.dot(block, up_w, preferred_element_type=jnp.float32)

    @pl.when(step == pl.num_programs(0) - 1)
    def _():
        out[...] = (jax.nn.silu(gate[...]) * up[...]).astype(out.dtype)


def swiglu(pieces, weights):
    rows = sum(n for p, n, place in pieces)
    width = pieces[0][0].shape[1]
    hidden = sum(w.shape[1] for w in weights) // 2
    depth = width // 7
    return pl.pallas_call(
        swiglu_kernel,
        out_shape=jax.ShapeDtypeStruct((rows, hidden), jnp.bfloat16),
        grid=(7,),
        in_specs=[
            pl.BlockSpec((n, depth), lambda i, place=place: (place, i))
            for p, n, place in pieces
        ]
        + [pl.BlockSpec((depth, w.shape[1]), lambda i: (i, 0)) for w in weights],
        out_specs=pl.BlockSpec((rows, hidden), lambda i: (0, 0)),
        scratch_shapes=[pltpu.VMEM((rows, hidden), jnp.float32)] * 2,
        compiler_params=pltpu.CompilerParams(vmem_limit_bytes=VMEM),
        cost_estimate=pl.CostEstimate(flops=1000, bytes_accessed=1000, transcendentals=0),
    )(*[p for p, n, place in pieces], *weights)


def down_kernel(own, by_x, by_y, across, mine, other, out, hidden):
    rows = own.shape[0] // 4
    half = own.shape[1] // 2

    @pl.when(pl.program_id(0) == 0)
    def _():
        for r, unit in enumerate((own, by_x, by_y, across)):
            for j in range(4):
                block = unit[(j ^ r) * rows : (j ^ r) * rows + rows]
                for h in range(2):
                    hidden[
                        j * rows : j * rows + rows, (h * 4 + r) * half : (h * 4 + r + 1) * half
                    ] = block[:, h * half : (h + 1) * half]

    total = jnp.dot(hidden[:, : 4 * half], mine[...], preferred_element_type=jnp.float32)
    total += jnp.dot(hidden[:, 4 * half :], other[...], preferred_element_type=jnp.float32)
    out[...] = total.astype(out.dtype)


def down(pieces, weights, vmem=VMEM):
    rows, hidden = pieces[0].shape
    width = weights[0].shape[1]
    cols = width // 2
    return pl.pallas_call(
        down_kernel,
        out_shape=jax.ShapeDtypeStruct((rows, width), jnp.bfloat16),
        grid=(2,),
        in_specs=[pl.BlockSpec(p.shape, lambda i: (0, 0)) for p in pieces]
        + [pl.BlockSpec((w.shape[0], cols), lambda i: (0, i)) for w in weights],
        out_specs=pl.BlockSpec((rows, cols), lambda i: (0, i)),
        scratch_shapes=[pltpu.VMEM((rows, 4 * hidden), jnp.bfloat16)],
        compiler_params=pltpu.CompilerParams(vmem_limit_bytes=vmem),
        cost_estimate=pl.CostEstimate(flops=1000, bytes_accessed=1000, transcendentals=0),
    )(*pieces, *weights)


def nothing(*refs):
    pass


def after(values, *earlier):
    values = tuple(values)
    return pl.pallas_call(
        nothing,
        out_shape=[jax.ShapeDtypeStruct(v.shape, v.dtype) for v in values],
        in_specs=[pl.BlockSpec(memory_space=pl.ANY)] * (len(values) + len(earlier)),
        out_specs=[pl.BlockSpec(memory_space=pl.ANY)] * len(values),
        input_output_aliases={i: i for i in range(len(values))},
        compiler_params=pltpu.CompilerParams(vmem_limit_bytes=2**20),
        cost_estimate=pl.CostEstimate(flops=0, bytes_accessed=0, transcendentals=0),
    )(*values, *earlier)


def four_planes(tokens, routes, probs, w_gate, w_up, w_down):
    rows, width = tokens.shape
    part = width // 4
    half = rows // 2
    me = lax.axis_index("node")
    z = me // GROUP
    quarter = me // 2 % 4
    chain = [jnp.zeros((8, 128), jnp.float32)]

    def gate(values, *earlier):
        chain[0], *values = after([chain[0], *values], *earlier)
        return values

    def cut(r):
        return lax.dynamic_slice_in_dim(w_down[0], (quarter ^ r) * part, part, axis=1)

    experts = jnp.arange(PLANES, dtype=jnp.int32)
    weights = jnp.sum(
        jnp.where(routes[:, :, None] == experts, probs[:, :, None], 0.0), axis=1
    )

    def join(*pieces):
        return jnp.concatenate(pieces, axis=0)

    def spread(hidden, *earlier):
        (hidden,) = gate([hidden], *earlier)
        return [hidden, swap(hidden, X), swap(hidden, Y), swap(hidden, X + Y)]

    def outputs(units, *earlier, split=False):
        (units[0],) = gate([units[0]], *earlier)
        out = down(units, down_w)
        return gate([out[: 2 * rows], out[2 * rows :]] if split else [out])

    col2, col1 = swap(tokens, 2 * Z), swap(tokens, Z)
    down_x, down_y, down_d = swap(cut(1), X), swap(cut(2), Y), swap(cut(3), X + Y)

    col2, down_x = gate([col2, down_x], col1, down_y, down_d)
    gate_a, up_a = gate([w_gate[0], w_up[0]])
    x2, y2, col3 = swap(col2, X), swap(col2, Y), swap(col2, Z)
    gate_b, up_b = swap(gate_a, CORE), swap(up_a, CORE)
    down_mine = jnp.concatenate([cut(0), down_x, down_y, down_d], axis=0)

    to_x, to_y, to_z, down_mine, w_0 = gate(
        [y2[half:], x2[:half], x2[:half], down_mine, weights], col3, gate_b, up_b
    )
    high2, low2, z_x_low = swap(to_x, X), swap(to_y, Y), swap(to_z, Z)
    down_w = [down_mine, swap(down_mine, CORE)]
    w_x = swap(w_0, X)
    swiglu_w = [w_gate[0], gate_b, w_up[0], up_b]

    col1, low2, w_0, to_z = gate(
        [col1, low2, w_0, x2[half:]], high2, down_w[1], w_x, z_x_low
    )
    x1, y1, z_x_high = swap(col1, X), swap(col1, Y), swap(to_z, Z)
    hidden_2 = swiglu(
        [(col2, rows, 0), (x2, rows, 0), (y2, rows, 0), (low2, half, 0), (high2, half, 0)],
        swiglu_w,
    )
    hidden_2, y2 = gate([hidden_2, y2], z_x_high)
    all_2 = [hidden_2, swap(hidden_2, X), swap(hidden_2, Y)]
    z_y = swap(y2, Z)
    x1, all_2[0] = gate([x1, all_2[0]], y1)
    all_2.append(swap(all_2[0], X + Y))

    to_x, to_y, to_z, all_2[0], w_0 = gate(
        [
            join(y1[half:], tokens[:half]),
            join(x1[:half], tokens[half:]),
            join(low2, high2),
            all_2[0],
            w_0,
        ],
        z_y,
        *all_2[1:],
    )
    x4, y4, zb = swap(to_x, X), swap(to_y, Y), swap(to_z, Z)
    w_y = swap(w_0, Y)
    first, second = outputs(all_2, split=True)
    back_2 = [swap(first, 2 * Z)]

    to_x, to_y, second, w_0 = gate(
        [tokens[half:], tokens[:half], second, w_0], zb, x4, y4, w_y
    )
    x5, y5 = swap(to_x, X), swap(to_y, Y)
    back_2.append(swap(second, 2 * Z))
    w_d = swap(w_0, X + Y)
    (mark,) = gate([col3])
    all_3 = spread(
        swiglu(
            [
                (mark, rows, 0),
                (z_x_low, half, 0),
                (z_x_high, half, 0),
                (z_y, rows, 0),
                (zb, rows, 0),
            ],
            swiglu_w,
        ),
        x5,
        y5,
        back_2[0],
    )
    (mark,) = gate([col1])
    hidden_1 = swiglu(
        [(mark, rows, 0), (x1, rows, 0), (y1, rows, 0), (y4, half, 0), (x4, half, 0)], swiglu_w
    )

    to_x, to_y, all_3[0], hidden_1 = gate(
        [y4[half:], x4[half:], all_3[0], hidden_1], w_d, back_2[1], *all_3[1:]
    )
    xe, ye = swap(to_x, X), swap(to_y, Y)
    (out_3,) = outputs(all_3)
    back_3 = [swap(out_3, 3 * Z)]
    all_1 = [hidden_1]

    xe, all_1[0] = gate([xe, all_1[0]], ye)
    all_1 = spread(all_1[0])
    all_0 = spread(
        swiglu(
            [
                (tokens, rows, 0),
                (x4, half, 1),
                (x5, half, 0),
                (y5, half, 0),
                (y4, half, 1),
                (ye, half, 0),
                (xe, half, 0),
            ],
            swiglu_w,
        )
    )
    (out_1,) = outputs(all_1, *all_1[1:])
    back_1 = [swap(out_1, Z)]
    (all_0[0],) = gate([all_0[0]], *all_0[1:])
    back_2 = [jnp.concatenate(back_2, axis=0)]
    weights = jnp.concatenate([w_0, w_x, w_y, w_d], axis=0)
    weights = jnp.concatenate(
        [
            jnp.sum(jnp.where(experts == (z ^ k), weights, 0.0), axis=1, keepdims=True)
            for k in range(PLANES)
        ],
        axis=1,
    )
    sums = [down(all_0, down_w, 56 * 2**20), back_1[0], back_2[0], back_3[0]]
    total = sum(weights[:, k : k + 1] * sums[k].astype(jnp.float32) for k in range(PLANES))
    mixed = total.astype(jnp.bfloat16).reshape(4, rows, part)
    pieces = [mixed[0], swap(mixed[1], X), swap(mixed[2], Y), swap(mixed[3], X + Y)]
    result = []
    for a in range(4):
        piece = pieces[a]
        for q in range(1, 4):
            piece = jnp.where(quarter == q, pieces[a ^ q], piece)
        result.append(piece)
    return jnp.concatenate(result, axis=1)


def solution(mesh):
    devices = mesh.shape["node"]

    def per_device(tokens, routes, probs, w_gate, w_up, w_down):
        path = four_planes if devices == COUNT else general
        return path(tokens, routes, probs, w_gate, w_up, w_down)

    in_specs = (
        P(("rep", "node"), None),
        P(("rep", "node"), None),
        P(("rep", "node"), None),
        P("node", None, None),
        P("node", None, None),
        P("node", None, None),
    )
    out_specs = P(("rep", "node"), None)
    return jax.shard_map(
        per_device, mesh=mesh, in_specs=in_specs, out_specs=out_specs, check_vma=False
    )
```

```python
import jax
import jax.numpy as jnp
from jax import lax
from jax.experimental import pallas as pl
from jax.experimental.pallas import tpu as pltpu
from jax.sharding import PartitionSpec as P

GROUP = 8
PLANES = 4


def general(tokens, routes, probs, w_gate, w_up, w_down):
    tok_rows, width = tokens.shape
    chosen_count = routes.shape[1]
    devices = lax.axis_size("node")
    experts = devices // GROUP
    slots = min(tok_rows, GROUP * max(1, 2 * tok_rows * chosen_count // (experts * GROUP)))
    flat_routes = routes.reshape(-1)
    onehot = (flat_routes[:, None] == jnp.arange(experts, dtype=jnp.int32)[None, :]).astype(
        jnp.int32
    )
    ranks = jnp.sum((jnp.cumsum(onehot, axis=0) - onehot) * onehot, axis=1)
    target = flat_routes * slots + ranks
    placed = target[:, None] == jnp.arange(experts * slots, dtype=jnp.int32)[None, :]
    placed = placed.reshape(tok_rows, chosen_count, experts * slots)
    sender = jnp.sum(placed.astype(jnp.float32), axis=1).astype(jnp.bfloat16)
    combine = jnp.sum(jnp.where(placed, probs[:, :, None], 0.0), axis=1)
    packed = lax.dot_general(
        sender, tokens, (((0,), (0,)), ((), ())), preferred_element_type=jnp.float32
    ).astype(jnp.bfloat16)
    spread = jnp.broadcast_to(
        packed.reshape(experts, 1, slots, width), (experts, GROUP, slots, width)
    )
    spread = spread.reshape(devices, slots, width)
    block = lax.all_to_all(spread, "node", split_axis=0, concat_axis=0, tiled=True)
    lead = block.shape[:-1]
    flat_rows = block.reshape(-1, width)
    gate = jnp.dot(flat_rows, w_gate[0], preferred_element_type=jnp.float32)
    up = jnp.dot(flat_rows, w_up[0], preferred_element_type=jnp.float32)
    hidden = (jax.nn.silu(gate) * up).astype(jnp.bfloat16)
    returned = lax.all_to_all(
        jnp.dot(hidden, w_down[0], preferred_element_type=jnp.float32).reshape(lead + (width,)),
        "node",
        split_axis=0,
        concat_axis=0,
        tiled=True,
    )
    summed = jnp.sum(returned.reshape(experts, GROUP, slots, width), axis=1).astype(jnp.bfloat16)
    mixed = jnp.dot(
        combine,
        summed.reshape(experts * slots, width).astype(jnp.float32),
        precision=lax.Precision.HIGHEST,
    )
    return mixed.astype(jnp.bfloat16)


CORE, X, Y, Z = 1, 2, 4, 8
COUNT = PLANES * GROUP


def swap(value, bits):
    return lax.ppermute(value, "node", [(i, i ^ bits) for i in range(COUNT)])


VMEM = 20 * 2**20


def swiglu_kernel(*refs):
    *pieces, gate_a, gate_b, up_a, up_b, out, gate, up = refs
    step = pl.program_id(0)

    @pl.when(step == 0)
    def _():
        gate[...] = jnp.zeros_like(gate)
        up[...] = jnp.zeros_like(up)

    block = jnp.concatenate([p[...] for p in pieces], axis=0)
    gate_w = jnp.concatenate([gate_a[...], gate_b[...]], axis=1)
    up_w = jnp.concatenate([up_a[...], up_b[...]], axis=1)
    gate[...] += jnp.dot(block, gate_w, preferred_element_type=jnp.float32)
    up[...] += jnp.dot(block, up_w, preferred_element_type=jnp.float32)

    @pl.when(step == pl.num_programs(0) - 1)
    def _():
        out[...] = (jax.nn.silu(gate[...]) * up[...]).astype(out.dtype)


def swiglu(pieces, weights):
    rows = sum(n for p, n, place in pieces)
    width = pieces[0][0].shape[1]
    hidden = sum(w.shape[1] for w in weights) // 2
    depth = width // 4
    return pl.pallas_call(
        swiglu_kernel,
        out_shape=jax.ShapeDtypeStruct((rows, hidden), jnp.bfloat16),
        grid=(4,),
        in_specs=[
            pl.BlockSpec((n, depth), lambda i, place=place: (place, i))
            for p, n, place in pieces
        ]
        + [pl.BlockSpec((depth, w.shape[1]), lambda i: (i, 0)) for w in weights],
        out_specs=pl.BlockSpec((rows, hidden), lambda i: (0, 0)),
        scratch_shapes=[pltpu.VMEM((rows, hidden), jnp.float32)] * 2,
        compiler_params=pltpu.CompilerParams(vmem_limit_bytes=VMEM),
        cost_estimate=pl.CostEstimate(flops=1000, bytes_accessed=1000, transcendentals=0),
    )(*[p for p, n, place in pieces], *weights)


def down_kernel(own, by_x, by_y, across, mine, other, out, hidden):
    rows = own.shape[0] // 4
    half = own.shape[1] // 2

    @pl.when(pl.program_id(0) == 0)
    def _():
        for r, unit in enumerate((own, by_x, by_y, across)):
            for j in range(4):
                block = unit[(j ^ r) * rows : (j ^ r) * rows + rows]
                for h in range(2):
                    hidden[
                        j * rows : j * rows + rows, (h * 4 + r) * half : (h * 4 + r + 1) * half
                    ] = block[:, h * half : (h + 1) * half]

    total = jnp.dot(hidden[:, : 4 * half], mine[...], preferred_element_type=jnp.float32)
    total += jnp.dot(hidden[:, 4 * half :], other[...], preferred_element_type=jnp.float32)
    out[...] = total.astype(out.dtype)


def down(pieces, weights, vmem=VMEM):
    rows, hidden = pieces[0].shape
    width = weights[0].shape[1]
    cols = width // 2
    return pl.pallas_call(
        down_kernel,
        out_shape=jax.ShapeDtypeStruct((rows, width), jnp.bfloat16),
        grid=(2,),
        in_specs=[pl.BlockSpec(p.shape, lambda i: (0, 0)) for p in pieces]
        + [pl.BlockSpec((w.shape[0], cols), lambda i: (0, i)) for w in weights],
        out_specs=pl.BlockSpec((rows, cols), lambda i: (0, i)),
        scratch_shapes=[pltpu.VMEM((rows, 4 * hidden), jnp.bfloat16)],
        compiler_params=pltpu.CompilerParams(vmem_limit_bytes=vmem),
        cost_estimate=pl.CostEstimate(flops=1000, bytes_accessed=1000, transcendentals=0),
    )(*pieces, *weights)


def nothing(*refs):
    pass


def after(values, *earlier):
    values = tuple(values)
    return pl.pallas_call(
        nothing,
        out_shape=[jax.ShapeDtypeStruct(v.shape, v.dtype) for v in values],
        in_specs=[pl.BlockSpec(memory_space=pl.ANY)] * (len(values) + len(earlier)),
        out_specs=[pl.BlockSpec(memory_space=pl.ANY)] * len(values),
        input_output_aliases={i: i for i in range(len(values))},
        compiler_params=pltpu.CompilerParams(vmem_limit_bytes=2**20),
        cost_estimate=pl.CostEstimate(flops=0, bytes_accessed=0, transcendentals=0),
    )(*values, *earlier)


def four_planes(tokens, routes, probs, w_gate, w_up, w_down):
    rows, width = tokens.shape
    part = width // 4
    half = rows // 2
    me = lax.axis_index("node")
    z = me // GROUP
    quarter = me // 2 % 4
    chain = [jnp.zeros((8, 128), jnp.float32)]

    def gate(values, *earlier):
        chain[0], *values = after([chain[0], *values], *earlier)
        return values

    def cut(r):
        return lax.dynamic_slice_in_dim(w_down[0], (quarter ^ r) * part, part, axis=1)

    experts = jnp.arange(PLANES, dtype=jnp.int32)
    weights = jnp.sum(
        jnp.where(routes[:, :, None] == experts, probs[:, :, None], 0.0), axis=1
    )

    def join(*pieces):
        return jnp.concatenate(pieces, axis=0)

    def spread(hidden, *earlier):
        (hidden,) = gate([hidden], *earlier)
        return [hidden, swap(hidden, X), swap(hidden, Y), swap(hidden, X + Y)]

    def outputs(units, *earlier, split=False):
        (units[0],) = gate([units[0]], *earlier)
        out = down(units, down_w)
        return gate([out[: 2 * rows], out[2 * rows :]] if split else [out])

    col2, col1 = swap(tokens, 2 * Z), swap(tokens, Z)
    down_x, down_y, down_d = swap(cut(1), X), swap(cut(2), Y), swap(cut(3), X + Y)

    col2, down_x = gate([col2, down_x], col1, down_y, down_d)
    gate_a, up_a = gate([w_gate[0], w_up[0]])
    x2, y2, col3 = swap(col2, X), swap(col2, Y), swap(col2, Z)
    gate_b, up_b = swap(gate_a, CORE), swap(up_a, CORE)
    down_mine = jnp.concatenate([cut(0), down_x, down_y, down_d], axis=0)

    to_x, to_y, to_z, down_mine, w_0 = gate(
        [y2[half:], x2[:half], x2[:half], down_mine, weights], col3, gate_b, up_b
    )
    high2, low2, z_x_low = swap(to_x, X), swap(to_y, Y), swap(to_z, Z)
    down_w = [down_mine, swap(down_mine, CORE)]
    w_x = swap(w_0, X)
    swiglu_w = [w_gate[0], gate_b, w_up[0], up_b]

    col1, low2, w_0, to_z = gate(
        [col1, low2, w_0, x2[half:]], high2, down_w[1], w_x, z_x_low
    )
    x1, y1, z_x_high = swap(col1, X), swap(col1, Y), swap(to_z, Z)
    hidden_2 = swiglu(
        [(col2, rows, 0), (x2, rows, 0), (y2, rows, 0), (low2, half, 0), (high2, half, 0)],
        swiglu_w,
    )
    hidden_2, y2 = gate([hidden_2, y2], z_x_high)
    all_2 = [hidden_2, swap(hidden_2, X), swap(hidden_2, Y)]
    z_y = swap(y2, Z)
    x1, all_2[0] = gate([x1, all_2[0]], y1)
    all_2.append(swap(all_2[0], X + Y))

    to_x, to_y, to_z, all_2[0], w_0 = gate(
        [
            join(y1[half:], tokens[:half]),
            join(x1[:half], tokens[half:]),
            join(low2, high2),
            all_2[0],
            w_0,
        ],
        z_y,
        *all_2[1:],
    )
    x4, y4, zb = swap(to_x, X), swap(to_y, Y), swap(to_z, Z)
    w_y = swap(w_0, Y)
    first, second = outputs(all_2, split=True)
    back_2 = [swap(first, 2 * Z)]

    to_x, to_y, second, w_0 = gate(
        [tokens[half:], tokens[:half], second, w_0], zb, x4, y4, w_y
    )
    x5, y5 = swap(to_x, X), swap(to_y, Y)
    back_2.append(swap(second, 2 * Z))
    w_d = swap(w_0, X + Y)
    (mark,) = gate([col3])
    all_3 = spread(
        swiglu(
            [
                (mark, rows, 0),
                (z_x_low, half, 0),
                (z_x_high, half, 0),
                (z_y, rows, 0),
                (zb, rows, 0),
            ],
            swiglu_w,
        ),
        x5,
        y5,
        back_2[0],
    )
    (mark,) = gate([col1])
    hidden_1 = swiglu(
        [(mark, rows, 0), (x1, rows, 0), (y1, rows, 0), (y4, half, 0), (x4, half, 0)], swiglu_w
    )

    to_x, to_y, all_3[0], hidden_1 = gate(
        [y4[half:], x4[half:], all_3[0], hidden_1], w_d, back_2[1], *all_3[1:]
    )
    xe, ye = swap(to_x, X), swap(to_y, Y)
    (out_3,) = outputs(all_3)
    back_3 = [swap(out_3, 3 * Z)]
    all_1 = [hidden_1]

    xe, all_1[0] = gate([xe, all_1[0]], ye)
    all_1 = spread(all_1[0])
    all_0 = spread(
        swiglu(
            [
                (tokens, rows, 0),
                (x4, half, 1),
                (x5, half, 0),
                (y5, half, 0),
                (y4, half, 1),
                (ye, half, 0),
                (xe, half, 0),
            ],
            swiglu_w,
        )
    )
    (out_1,) = outputs(all_1, *all_1[1:])
    back_1 = [swap(out_1, Z)]
    (all_0[0],) = gate([all_0[0]], *all_0[1:])
    back_2 = [jnp.concatenate(back_2, axis=0)]
    weights = jnp.concatenate([w_0, w_x, w_y, w_d], axis=0)
    weights = jnp.concatenate(
        [
            jnp.sum(jnp.where(experts == (z ^ k), weights, 0.0), axis=1, keepdims=True)
            for k in range(PLANES)
        ],
        axis=1,
    )
    sums = [down(all_0, down_w, 56 * 2**20), back_1[0], back_2[0], back_3[0]]
    total = sum(weights[:, k : k + 1] * sums[k].astype(jnp.float32) for k in range(PLANES))
    mixed = total.astype(jnp.bfloat16).reshape(4, rows, part)
    pieces = [mixed[0], swap(mixed[1], X), swap(mixed[2], Y), swap(mixed[3], X + Y)]
    result = []
    for a in range(4):
        piece = pieces[a]
        for q in range(1, 4):
            piece = jnp.where(quarter == q, pieces[a ^ q], piece)
        result.append(piece)
    return jnp.concatenate(result, axis=1)


def solution(mesh):
    devices = mesh.shape["node"]

    def per_device(tokens, routes, probs, w_gate, w_up, w_down):
        path = four_planes if devices == COUNT else general
        return path(tokens, routes, probs, w_gate, w_up, w_down)

    in_specs = (
        P(("rep", "node"), None),
        P(("rep", "node"), None),
        P(("rep", "node"), None),
        P("node", None, None),
        P("node", None, None),
        P("node", None, None),
    )
    out_specs = P(("rep", "node"), None)
    return jax.shard_map(
        per_device, mesh=mesh, in_specs=in_specs, out_specs=out_specs, check_vma=False
    )
```
